256 devices in a mesh: vir: 32 (over x, z), occ: 8 (over y, core).
Axes of the slice: x: 4, y: 4, z: 8, core: 2. Of those that a mesh axis runs over, the one named last changes fastest.
Arguments:
- amplitudes: bfloat16 [65536, 6144], P('vir', 'occ'), may hold values from -6 to 6
- integrals: bfloat16 [8192, 128, 128], P(('vir', 'occ')), may hold values from -0.25 to 0.25
- task_block: int32 [8192], P('vir'), may hold values from 0 to 15
- task_source: int32 [8192], P('vir'), may hold values from 0 to 63
- task_count: int32 [32], P('vir'), may hold values from 128 to 256, as said below
Outputs:
- ladder: bfloat16 [65536, 6144], P('vir', 'occ')
The draws below stay inside these ranges and needn't reach their ends.
Inputs may be any that keep to these rules, and one draw needn't show every extreme that they name: Vir index v's live tasks are its slots 0 to task_count[v] - 1; the other slots hold no task. Some vir index has all 256 slots live.
All inputs are finite; a program needn't handle non-finite values.
Results may differ from the reference program's by a relative error of at most 0.001.
Values may be sent and summed in bfloat16 or wider, within the bound.
A program may use at most 128 MiB of HBM per device.

```python
import jax
import jax.numpy as jnp
from jax import lax

TILE = 128
GROUP = 4
BLK_DEV = 16
TASK_DEV = 256
VPAIRS = 65536
PAIRS = 6144
NTASK = 8192
GBLK = 64
N_VIR = 32


def draw_task_count(key, part):
    key = jax.random.fold_in(key, 7)
    count_key, heavy_key = jax.random.split(key)
    counts = jax.random.randint(count_key, (N_VIR,), TASK_DEV // 2, 3 * TASK_DEV // 4 + 1)
    busiest = jax.random.randint(heavy_key, (), 0, N_VIR)
    return jnp.where(jnp.arange(N_VIR) == busiest, TASK_DEV, counts).astype(jnp.int32)


def set_ends(array, own_key, least, largest):
    spot = [jax.random.randint(jax.random.fold_in(own_key, axis), (), 0, length) for axis, length in enumerate(array.shape)]
    longest = array.shape.index(max(array.shape))
    neighbour = spot[:longest] + [(spot[longest] + 1) % array.shape[longest]] + spot[longest + 1:]
    return array.at[tuple(spot)].set(least).at[tuple(neighbour)].set(largest)


def level_of(stream_key, dims, shards, least, largest):
    level, own = 1.0, jax.random.fold_in(stream_key, 6)
    for dim, parts in shards:
        steps = jnp.exp(jax.random.uniform(jax.random.fold_in(own, dim), (parts,), jnp.float32, least / len(shards), largest / len(shards)))
        level = level * jnp.repeat(steps, dims[dim] // parts).reshape([-1 if axis == dim else 1 for axis in range(len(dims))])
    return level


def bell_draw(stream_key, shape, width, bound, shards=(), kind=jnp.bfloat16):
    loudness = level_of(stream_key, shape, shards, -0.22, 0.18) if shards else 1.0
    entries = jax.random.normal(stream_key, shape, jnp.float32) * width * loudness
    return jnp.minimum(jnp.maximum(entries, -bound), bound).astype(kind)


def setup_inputs(seed: int = 0) -> dict:
    streams_of = jax.random.split(jax.random.key(seed), 6)
    return {
        "amplitudes": bell_draw(streams_of[0], (VPAIRS, PAIRS), 1.0, 6.0, ((0, 32), (1, 8))),
        "integrals": bell_draw(streams_of[1], (NTASK, TILE, TILE), (4 * TILE) ** -0.5, 0.25, ((0, 256),)),
        "task_block": set_ends(jax.random.randint(streams_of[2], (NTASK,), 0, BLK_DEV), jax.random.fold_in(streams_of[2], 1), 0, BLK_DEV - 1).astype(jnp.int32),
        "task_source": set_ends(jax.random.randint(streams_of[3], (NTASK,), 0, GBLK), jax.random.fold_in(streams_of[3], 1), 0, GBLK - 1).astype(jnp.int32),
        "task_count": draw_task_count(jax.random.fold_in(streams_of[5], 71), 0),
    }


def reference(amplitudes, integrals, task_block, task_source, task_count):
    grouped = amplitudes.reshape(N_VIR // GROUP, GROUP * BLK_DEV, TILE, PAIRS)
    tile_table = integrals.reshape(N_VIR, TASK_DEV, TILE, TILE)
    blocks = task_block.reshape(N_VIR, TASK_DEV)
    sources = task_source.reshape(N_VIR, TASK_DEV)

    def per_device(device_index):
        group_rows = lax.dynamic_index_in_dim(grouped, device_index // GROUP, 0, keepdims=False)
        own_tiles = lax.dynamic_index_in_dim(tile_table, device_index, 0, keepdims=False)
        own_blocks = lax.dynamic_index_in_dim(blocks, device_index, 0, keepdims=False)
        own_sources = lax.dynamic_index_in_dim(sources, device_index, 0, keepdims=False)
        live_total = lax.dynamic_index_in_dim(task_count, device_index, 0, keepdims=False)

        def slot_step(accumulated, slot_index):
            live_flag = (slot_index < live_total).astype(jnp.float32)
            tile_now = lax.dynamic_index_in_dim(own_tiles, slot_index, 0, keepdims=False)
            source_index = lax.dynamic_index_in_dim(own_sources, slot_index, 0, keepdims=False)
            block_index = lax.dynamic_index_in_dim(own_blocks, slot_index, 0, keepdims=False)
            source_rows = lax.dynamic_index_in_dim(group_rows, source_index, 0, keepdims=False)
            product_term = jnp.dot(tile_now, source_rows, preferred_element_type=jnp.float32) * live_flag
            current = lax.dynamic_index_in_dim(accumulated, block_index, 0, keepdims=True)
            accumulated = lax.dynamic_update_index_in_dim(accumulated, current + product_term[None], block_index, 0)
            return accumulated, None

        start_sum = jnp.zeros((BLK_DEV, TILE, PAIRS), jnp.float32)
        accumulated, _ = lax.scan(slot_step, start_sum, jnp.arange(TASK_DEV, dtype=jnp.int32))
        return accumulated.astype(jnp.bfloat16)

    stacked = lax.map(per_device, jnp.arange(N_VIR, dtype=jnp.int32))
    return stacked.reshape(VPAIRS, PAIRS)
```

```python
import functools

import jax
import jax.numpy as jnp
from jax import lax
from jax.sharding import PartitionSpec as P
import jax.experimental.pallas as pl
import jax.experimental.pallas.tpu as pltpu

MESH = pl.DeviceIdType.MESH
ZLEN = 8
GROUP = 4
YLEN = 4
TILE = 128
BLOCKS = 16
SLOTS = 256
SHARD = 32
PAIRS = (SLOTS + BLOCKS) // 2
ROW = 384
WIDTHS = (128, 128, 256, 128, 128)
STARTS = (0, 128, 256, 512, 640)
N = len(WIDTHS)
UNROLL = 8


def task_table(count, block, source):
    i32 = jnp.int32
    slot_l = lax.broadcasted_iota(i32, (SLOTS, SLOTS), 1)
    slot_s = lax.broadcasted_iota(i32, (SLOTS, SLOTS), 0)
    key_l = jnp.where(slot_l < count, jnp.broadcast_to(block, (SLOTS, SLOTS)), BLOCKS)
    key_s = key_l.T
    source_s = jnp.broadcast_to(source, (SLOTS, SLOTS)).T[:, 0:1]
    before = jnp.where((key_l == key_s) & (slot_l < slot_s), 1, 0)
    order = jnp.sum(before, axis=1, keepdims=True)
    key = key_s[:, 0:1]
    blk_s = lax.broadcasted_iota(i32, (BLOCKS, SLOTS), 0)
    n_s = jnp.sum(jnp.where(key_l[0:BLOCKS] == blk_s, 1, 0), axis=1, keepdims=True)
    even_s = ((n_s + 1) // 2) * 2
    lane = lax.broadcasted_iota(i32, (SLOTS, ROW), 1)
    n_l = jnp.sum(jnp.where(key == lane, 1, 0), axis=0, keepdims=True)
    n_l = jnp.where(lane[0:1] < BLOCKS, n_l, 0)
    even_l = ((n_l + 1) // 2) * 2
    lane16 = lax.broadcasted_iota(i32, (BLOCKS, ROW), 1)
    sub16 = lax.broadcasted_iota(i32, (BLOCKS, ROW), 0)
    base_l = jnp.sum(jnp.where(sub16 < lane16, even_s, 0), axis=0, keepdims=True)
    base_s = jnp.sum(jnp.where(lane16 < sub16, even_l, 0), axis=1, keepdims=True)
    base = jnp.sum(jnp.where(lane < key, even_l, 0), axis=1, keepdims=True)
    place = jnp.where(key < BLOCKS, base + order, ROW)
    here = place == lane
    slot = lax.broadcasted_iota(i32, (SLOTS, ROW), 0)
    amp = jnp.sum(jnp.where(here, source_s, 0), axis=0, keepdims=True)
    integral = SLOTS + jnp.sum(jnp.where(here, slot - SLOTS, 0), axis=0, keepdims=True)
    begins = jnp.where((base_s == 2 * lane16) & (n_s > 0), 1, 0)
    goes_on = 1 - jnp.sum(begins, axis=0, keepdims=True)
    last = jnp.maximum((base_l + even_l) // 2 - 1, 0)
    last = jnp.where(lane[0:1] < BLOCKS, last, 0)
    filled = jnp.where(n_l > 0, 1, 0)
    row = lax.broadcasted_iota(i32, (8, ROW), 0)
    out = jnp.where(row == 0, amp, 0)
    for k, value in ((1, integral), (2, goes_on), (3, last), (4, filled)):
        out = jnp.where(row == k, value, out)
    return out


def kernel(amp_ref, int_ref, block_ref, source_ref, count_ref, out_ref, *scratch):
    held = scratch[0:N]
    done = scratch[N : 2 * N]
    mine = scratch[2 * N : 3 * N]
    (tiles_own, tiles_out, prefix, table_own, table_out, smem_own, smem_out,
     s_own, r_own, s_fwd, r_fwd, s_amp, r_amp, s_res, r_res, l_amp, l_out,
     s_ring, r_ring, s_half, r_half, s_core, r_core, s_v, r_v, s_tab, r_tab,
     l_v, l_tab) = scratch[3 * N :]
    tiles = (tiles_own, tiles_out)

    vir = lax.axis_index("vir")
    occ = lax.axis_index("occ")
    pos = vir % GROUP
    first = vir - pos
    y, core = occ // 2, occ % 2
    inner = (pos == 1) | (pos == 2)
    partner_pos = jnp.where(pos < 2, 1 - pos, 5 - pos)
    partner = (first + partner_pos, occ)
    cross_pos = 3 - pos
    cross = (first + cross_pos, occ)
    cross_partner_pos = jnp.where(cross_pos < 2, 1 - cross_pos, 5 - cross_pos)
    y_up = (vir, ((y + 1) % YLEN) * 2 + core)
    y_down = (vir, ((y + 3) % YLEN) * 2 + core)
    other = (vir, y * 2 + 1 - core)

    def part(ref, where):
        return ref.at[pl.ds(where * BLOCKS, BLOCKS)]

    def shard(p, yy, cc, begin=0, size=SHARD):
        start = ((yy % YLEN) * 2 + cc) * SHARD + begin
        return tiles[p].at[pl.ds(start, size)]

    def columns(ref, c):
        return ref.at[:, :, pl.ds(STARTS[c], WIDTHS[c])]

    def send(src, dst, ssem, rsem, to):
        return pltpu.make_async_remote_copy(
            src_ref=src, dst_ref=dst, send_sem=ssem, recv_sem=rsem, device_id=to, device_id_type=MESH
        )

    barrier = pltpu.get_barrier_semaphore()

    def load_amp(c):
        return pltpu.make_async_copy(columns(amp_ref, c), part(held[c], pos), l_amp.at[c])

    def amp_in(c, where):
        return send(part(held[c], where), part(held[c], where), s_amp.at[c], r_amp.at[c], partner)

    def v_in():
        return send(int_ref, shard(1, y, core), s_v, r_v, partner)

    def tab_in():
        return send(table_own, table_out, s_tab, r_tab, partner)

    def result(c, where):
        return send(done[c], part(held[c], where), s_res.at[c], r_res.at[c], partner)

    @pl.when(jnp.logical_not(inner))
    def _():
        pl.semaphore_signal(barrier, inc=1, device_id=partner, device_id_type=MESH)
        for c in range(N):
            load_amp(c).start()
        table_own[...] = task_table(count_ref[0], block_ref[...], source_ref[...])
        pl.semaphore_wait(barrier, 1)
        tab_in().start()
        v_in().start()
        queue = [v_in()]
        for c in range(N):
            load_amp(c).wait()
            if len(queue) > 1:
                queue.pop(0).wait_send()
            copy = amp_in(c, pos)
            copy.start()
            queue.append(copy)
        for copy in queue:
            copy.wait_send()
        tab_in().wait_send()
        for c in range(N):
            result(c, partner_pos).wait_recv()
            pltpu.make_async_copy(part(held[c], partner_pos), columns(out_ref, c), l_out.at[c]).start()
        for c in range(N):
            pltpu.make_async_copy(part(held[c], partner_pos), columns(out_ref, c), l_out.at[c]).wait()

    @pl.when(inner)
    def _():
        for to in (partner, cross, y_up, y_down, other):
            pl.semaphore_signal(barrier, inc=1, device_id=to, device_id_type=MESH)
        for c in range(N):
            load_amp(c).start()
        load_v = pltpu.make_async_copy(int_ref, shard(0, y, core), l_v)
        load_v.start()
        pl.semaphore_wait(barrier, 5)

        def own(c):
            return send(part(held[c], pos), part(held[c], pos), s_own.at[c], r_own.at[c], cross)

        def own_in(c):
            return send(part(held[c], pos), part(held[c], cross_pos), s_own.at[c], r_own.at[c], cross)

        def fwd(c):
            return send(part(held[c], partner_pos), part(held[c], partner_pos), s_fwd.at[c], r_fwd.at[c], cross)

        def fwd_in(c):
            return send(part(held[c], partner_pos), part(held[c], cross_partner_pos), s_fwd.at[c], r_fwd.at[c], cross)

        def ring(p, way, src=None):
            src = shard(p, y, core) if src is None else src
            return send(src, shard(p, y, core), s_ring.at[p, way], r_ring.at[p, way], (y_up, y_down)[way])

        def ring_in(p, way):
            return send(shard(p, y, core), shard(p, y + (3, 1)[way], core), s_ring.at[p, way], r_ring.at[p, way],
                        (y_up, y_down)[way])

        def half(p, way):
            ref = shard(p, y + (3, 1)[way], core, way * (SHARD // 2), SHARD // 2)
            return send(ref, ref, s_half.at[p, way], r_half.at[p, way], (y_up, y_down)[way])

        def half_in(p, way):
            ref = shard(p, y + 2, core, way * (SHARD // 2), SHARD // 2)
            return send(ref, ref, s_half.at[p, way], r_half.at[p, way], (y_up, y_down)[way])

        def swap(p, turn, src=None):
            ref = shard(p, y + turn, core)
            return send(ref if src is None else src, ref, s_core.at[p, turn], r_core.at[p, turn], other)

        def swap_in(p, turn):
            return send(shard(p, y + turn, core), shard(p, y + turn, 1 - core), s_core.at[p, turn],
                        r_core.at[p, turn], other)

        def ring_on(p):
            for way in range(2):
                ring_in(p, way).wait_recv()
                half(p, way).start()
                swap(p, (3, 1)[way]).start()

        def ring_end(p):
            for way in range(2):
                half_in(p, way).wait_recv()
            swap(p, 2).start()
            for turn in range(YLEN):
                swap_in(p, turn).wait_recv()

        load_amp(0).wait()
        own(0).start()
        ring(0, 0, int_ref).start()
        ring(0, 1, int_ref).start()
        load_amp(1).wait()
        own(1).start()
        load_amp(2).wait()
        own(2).start()
        swap(0, 0, int_ref).start()

        tiles_own[SLOTS] = jnp.zeros((TILE, TILE), jnp.bfloat16)
        tiles_out[SLOTS] = jnp.zeros((TILE, TILE), jnp.bfloat16)
        table_own[...] = task_table(count_ref[0], block_ref[...], source_ref[...])
        tab_a = pltpu.make_async_copy(table_own, smem_own, l_tab.at[0])
        tab_a.start()
        tab_in().wait_recv()
        tab_b = pltpu.make_async_copy(table_out, smem_out, l_tab.at[1])
        tab_b.start()
        load_v.wait()
        tab_a.wait()
        tab_b.wait()
        for c in range(3, N):
            load_amp(c).wait()

        def compute(c, p):
            width = WIDTHS[c]
            smem = (smem_own, smem_out)[p]
            target = (mine, done)[p][c]

            def pair(j, total):
                a, b = 2 * j, 2 * j + 1
                left = jnp.concatenate([tiles[p][smem[1, a]], tiles[p][smem[1, b]]], 1)
                right = jnp.concatenate([held[c][smem[0, a]], held[c][smem[0, b]]], 0)
                product = jnp.dot(left, right, preferred_element_type=jnp.float32)
                total = total * smem[2, j].astype(jnp.float32) + product
                prefix[j, :, 0:width] = total.astype(jnp.bfloat16)
                return total

            lax.fori_loop(0, PAIRS, pair, jnp.zeros((TILE, width), jnp.float32), unroll=UNROLL)

            def place(b, carry):
                value = prefix[smem[3, b], :, 0:width].astype(jnp.float32)
                target[b] = (value * smem[4, b].astype(jnp.float32)).astype(jnp.bfloat16)
                return carry

            lax.fori_loop(0, BLOCKS, place, 0)
            if p:
                result(c, pos).start()
            else:
                pltpu.make_async_copy(target, columns(out_ref, c), l_out.at[c]).start()

        def issue_fwd(c):
            amp_in(c, partner_pos).wait_recv()
            fwd(c).start()

        def chunk_in(c):
            own_in(c).wait_recv()
            fwd_in(c).wait_recv()

        ring_on(0)
        v_in().wait_recv()
        ring(1, 0).start()
        ring(1, 1).start()
        swap(1, 0).start()
        own(0).wait_send()
        issue_fwd(0)
        own(1).wait_send()
        issue_fwd(1)
        ring_end(0)
        own(2).wait_send()
        issue_fwd(2)
        ring_on(1)
        chunk_in(0)
        compute(0, 0)
        fwd(0).wait_send()
        own(3).start()
        ring_end(1)
        compute(0, 1)
        chunk_in(1)
        compute(1, 1)
        fwd(1).wait_send()
        issue_fwd(3)
        compute(1, 0)
        fwd(2).wait_send()
        own(4).start()
        chunk_in(2)
        compute(2, 1)
        own(3).wait_send()
        issue_fwd(4)
        compute(2, 0)
        chunk_in(3)
        compute(3, 1)
        compute(3, 0)
        chunk_in(4)
        compute(4, 1)
        compute(4, 0)

        fwd(3).wait_send()
        own(4).wait_send()
        fwd(4).wait_send()
        for p in range(2):
            for way in range(2):
                ring(p, way).wait_send()
                half(p, way).wait_send()
            for turn in range(YLEN):
                swap(p, turn).wait_send()
        for c in range(N):
            result(c, pos).wait_send()
            pltpu.make_async_copy(mine[c], columns(out_ref, c), l_out.at[c]).wait()


def local(amplitudes, integrals, task_block, task_source, task_count):
    pair_count = amplitudes.shape[1]
    dma = pltpu.SemaphoreType.DMA
    bf16 = jnp.bfloat16
    chunks = [pltpu.VMEM((BLOCKS, TILE, w), bf16) for w in WIDTHS]
    scratch = [pltpu.VMEM((GROUP * BLOCKS, TILE, w), bf16) for w in WIDTHS] + chunks + chunks
    scratch += [
        pltpu.VMEM((SLOTS + 1, TILE, TILE), bf16),
        pltpu.VMEM((SLOTS + 1, TILE, TILE), bf16),
        pltpu.VMEM((PAIRS, TILE, max(WIDTHS)), bf16),
        pltpu.VMEM((8, ROW), jnp.int32),
        pltpu.VMEM((8, ROW), jnp.int32),
        pltpu.SMEM((8, ROW), jnp.int32),
        pltpu.SMEM((8, ROW), jnp.int32),
    ]
    scratch += [dma((N,))] * 10
    scratch += [dma((2, 2))] * 4 + [dma((2, YLEN))] * 2 + [dma] * 5 + [dma((2,))]
    any_space = pl.BlockSpec(memory_space=pl.ANY)
    vmem = pl.BlockSpec(memory_space=pltpu.VMEM)
    smem = pl.BlockSpec(memory_space=pltpu.SMEM)
    result = pl.pallas_call(
        kernel,
        name="ladder",
        out_shape=jax.ShapeDtypeStruct((BLOCKS, TILE, pair_count), bf16),
        in_specs=[any_space, any_space, vmem, vmem, smem],
        out_specs=any_space,
        scratch_shapes=scratch,
        compiler_params=pltpu.CompilerParams(
            collective_id=0, has_side_effects=True, vmem_limit_bytes=60 * 2**20
        ),
        cost_estimate=pl.CostEstimate(
            flops=4 * SLOTS * TILE * TILE * pair_count, bytes_accessed=8 * 2**20, transcendentals=0
        ),
    )(
        amplitudes.reshape(BLOCKS, TILE, pair_count),
        integrals,
        task_block.reshape(1, SLOTS),
        task_source.reshape(1, SLOTS),
        task_count,
    )
    return result.reshape(BLOCKS * TILE, pair_count)


def solution(mesh):
    return jax.shard_map(
        local,
        mesh=mesh,
        in_specs=(P("vir", "occ"), P(("vir", "occ"), None, None), P("vir"), P("vir"), P("vir")),
        out_specs=P("vir", "occ"),
        check_vma=False,
    )
```

```python
import functools

import jax
import jax.numpy as jnp
from jax import lax
from jax.sharding import PartitionSpec as P
import jax.experimental.pallas as pl
import jax.experimental.pallas.tpu as pltpu

MESH = pl.DeviceIdType.MESH
ZLEN = 8
GROUP = 4
YLEN = 4
TILE = 128
HALF = TILE // 2
BLOCKS = 16
SLOTS = 256
SHARD = 32
PAIRS = (SLOTS + BLOCKS) // 2
ROW = 384
WIDTHS = (128,) * 6
STARTS = (0, 128, 256, 384, 512, 640)
N = len(WIDTHS)
UNROLL = 17
UNROLL_LAST = 34


def task_table(count, block, source):
    i32 = jnp.int32
    slot_l = lax.broadcasted_iota(i32, (SLOTS, SLOTS), 1)
    slot_s = lax.broadcasted_iota(i32, (SLOTS, SLOTS), 0)
    key_l = jnp.where(slot_l < count, jnp.broadcast_to(block, (SLOTS, SLOTS)), BLOCKS)
    key_s = key_l.T
    source_s = jnp.broadcast_to(source, (SLOTS, SLOTS)).T[:, 0:1]
    before = jnp.where((key_l == key_s) & (slot_l < slot_s), 1, 0)
    order = jnp.sum(before, axis=1, keepdims=True)
    key = key_s[:, 0:1]
    blk_s = lax.broadcasted_iota(i32, (BLOCKS, SLOTS), 0)
    n_s = jnp.sum(jnp.where(key_l[0:BLOCKS] == blk_s, 1, 0), axis=1, keepdims=True)
    even_s = ((n_s + 1) // 2) * 2
    lane = lax.broadcasted_iota(i32, (SLOTS, ROW), 1)
    n_l = jnp.sum(jnp.where(key == lane, 1, 0), axis=0, keepdims=True)
    n_l = jnp.where(lane[0:1] < BLOCKS, n_l, 0)
    even_l = ((n_l + 1) // 2) * 2
    lane16 = lax.broadcasted_iota(i32, (BLOCKS, ROW), 1)
    sub16 = lax.broadcasted_iota(i32, (BLOCKS, ROW), 0)
    base_l = jnp.sum(jnp.where(sub16 < lane16, even_s, 0), axis=0, keepdims=True)
    base_s = jnp.sum(jnp.where(lane16 < sub16, even_l, 0), axis=1, keepdims=True)
    base = jnp.sum(jnp.where(lane < key, even_l, 0), axis=1, keepdims=True)
    place = jnp.where(key < BLOCKS, base + order, ROW)
    here = place == lane
    slot = lax.broadcasted_iota(i32, (SLOTS, ROW), 0)
    amp = jnp.sum(jnp.where(here, source_s, 0), axis=0, keepdims=True)
    integral = SLOTS + jnp.sum(jnp.where(here, slot - SLOTS, 0), axis=0, keepdims=True)
    begins = jnp.where((base_s == 2 * lane16) & (n_s > 0), 1, 0)
    goes_on = 1 - jnp.sum(begins, axis=0, keepdims=True)
    last = jnp.maximum((base_l + even_l) // 2 - 1, 0)
    last = jnp.where(lane[0:1] < BLOCKS, last, 0)
    filled = jnp.where(n_l > 0, 1, 0)
    row = lax.broadcasted_iota(i32, (8, ROW), 0)
    out = jnp.where(row == 0, amp, 0)
    for k, value in ((1, integral), (2, goes_on), (3, last), (4, filled)):
        out = jnp.where(row == k, value, out)
    return out


def kernel(amp_ref, int_ref, block_hbm, source_hbm, count_ref, out_ref, *scratch):
    held = scratch[0:N]
    done = scratch[N : 2 * N]
    mine = scratch[2 * N : 3 * N]
    (tiles_own, tiles_out, prefix, table_own, table_out, smem_own, smem_out,
     s_own, r_own, s_fwd, r_fwd, s_amp, r_amp, s_res, r_res, l_amp, l_out,
     s_ring, r_ring, s_half, r_half, s_core, r_core, s_v, r_v, s_tab, r_tab,
     l_v, l_tab, turn_sem, block_ref, source_ref, l_list, s_part, r_part) = scratch[3 * N :]
    tiles = (tiles_own, tiles_out)

    vir = lax.axis_index("vir")
    occ = lax.axis_index("occ")
    pos = vir % GROUP
    first = vir - pos
    y, core = occ // 2, occ % 2
    inner = (pos == 1) | (pos == 2)
    partner_pos = jnp.where(pos < 2, 1 - pos, 5 - pos)
    partner = (first + partner_pos, occ)
    cross_pos = 3 - pos
    cross = (first + cross_pos, occ)
    cross_partner_pos = jnp.where(cross_pos < 2, 1 - cross_pos, 5 - cross_pos)
    y_up = (vir, ((y + 1) % YLEN) * 2 + core)
    y_down = (vir, ((y + 3) % YLEN) * 2 + core)
    other = (vir, y * 2 + 1 - core)

    def part(ref, where):
        return ref.at[pl.ds(where * BLOCKS, BLOCKS)]

    def shard(p, yy, cc, begin=0, size=SHARD):
        start = ((yy % YLEN) * 2 + cc) * SHARD + begin
        return tiles[p].at[pl.ds(start, size)]

    def columns(ref, c):
        return ref.at[:, :, pl.ds(STARTS[c], WIDTHS[c])]

    def send(src, dst, ssem, rsem, to):
        return pltpu.make_async_remote_copy(
            src_ref=src, dst_ref=dst, send_sem=ssem, recv_sem=rsem, device_id=to, device_id_type=MESH
        )

    barrier = pltpu.get_barrier_semaphore()
    lists = [
        pltpu.make_async_copy(block_hbm, block_ref, l_list.at[0]),
        pltpu.make_async_copy(source_hbm, source_ref, l_list.at[1]),
    ]

    def make_table():
        for copy in lists:
            copy.wait()
        table_own[...] = task_table(count_ref[0], block_ref[...], source_ref[...])

    def load_amp(c):
        return pltpu.make_async_copy(columns(amp_ref, c), part(held[c], pos), l_amp.at[c])

    def amp_in(c, where):
        return send(part(held[c], where), part(held[c], where), s_amp.at[c], r_amp.at[c], partner)

    def v_in():
        return send(int_ref, shard(1, y, core), s_v, r_v, partner)

    def tab_in():
        return send(table_own, table_out, s_tab, r_tab, partner)

    def result(c):
        return send(done[c], columns(out_ref, c), s_res.at[c], r_res.at[c], partner)

    def result_part(c, top, rows):
        k = top // rows
        return send(done[c].at[:, pl.ds(top, rows)], columns(out_ref, c).at[:, pl.ds(top, rows)],
                    s_part.at[k], r_part.at[k], partner)

    @pl.when(jnp.logical_not(inner))
    def _():
        pl.semaphore_signal(barrier, inc=1, device_id=partner, device_id_type=MESH)
        for c in range(N):
            load_amp(c).start()
        for copy in lists:
            copy.start()
        pl.semaphore_wait(barrier, 1)
        v_in().start()
        make_table()
        tab_in().start()
        v_in().wait_send()
        queue = []
        for c in range(N):
            load_amp(c).wait()
            if len(queue) > 1:
                queue.pop(0).wait_send()
            copy = amp_in(c, pos)
            copy.start()
            queue.append(copy)
        for copy in queue:
            copy.wait_send()
        tab_in().wait_send()
        for c in range(N - 1):
            result(c).wait_recv()
        for k in range(2):
            result_part(N - 1, k * HALF, HALF).wait_recv()

    @pl.when(inner)
    def _():
        for to in (partner, cross, y_up, y_down, other):
            pl.semaphore_signal(barrier, inc=1, device_id=to, device_id_type=MESH)
        for c in range(N):
            load_amp(c).start()
        load_v = pltpu.make_async_copy(int_ref, shard(0, y, core), l_v)
        load_v.start()
        for copy in lists:
            copy.start()
        pl.semaphore_wait(barrier, 5)

        def own(c):
            return send(part(held[c], pos), part(held[c], pos), s_own.at[c], r_own.at[c], cross)

        def own_in(c):
            return send(part(held[c], pos), part(held[c], cross_pos), s_own.at[c], r_own.at[c], cross)

        def fwd(c):
            return send(part(held[c], partner_pos), part(held[c], partner_pos), s_fwd.at[c], r_fwd.at[c], cross)

        def fwd_in(c):
            return send(part(held[c], partner_pos), part(held[c], cross_partner_pos), s_fwd.at[c], r_fwd.at[c], cross)

        def ring(p, way, src=None):
            src = shard(p, y, core) if src is None else src
            return send(src, shard(p, y, core), s_ring.at[p, way], r_ring.at[p, way], (y_up, y_down)[way])

        def ring_in(p, way):
            return send(shard(p, y, core), shard(p, y + (3, 1)[way], core), s_ring.at[p, way], r_ring.at[p, way],
                        (y_up, y_down)[way])

        def half(p, way):
            ref = shard(p, y + (3, 1)[way], core, way * (SHARD // 2), SHARD // 2)
            return send(ref, ref, s_half.at[p, way], r_half.at[p, way], (y_up, y_down)[way])

        def half_in(p, way):
            ref = shard(p, y + 2, core, way * (SHARD // 2), SHARD // 2)
            return send(ref, ref, s_half.at[p, way], r_half.at[p, way], (y_up, y_down)[way])

        def swap(p, turn, src=None):
            ref = shard(p, y + turn, core)
            return send(ref if src is None else src, ref, s_core.at[p, turn], r_core.at[p, turn], other)

        def swap_in(p, turn):
            return send(shard(p, y + turn, core), shard(p, y + turn, 1 - core), s_core.at[p, turn],
                        r_core.at[p, turn], other)

        def ring_come(p):
            for way in range(2):
                ring_in(p, way).wait_recv()
                swap(p, (3, 1)[way]).start()

        def ring_on(p):
            for way in range(2):
                half(p, way).start()

        def ring_end(p):
            for way in range(2):
                half_in(p, way).wait_recv()
            swap(p, 2).start()

        def swap_end(p):
            for turn in range(YLEN):
                swap_in(p, turn).wait_recv()

        load_amp(0).wait()
        own(0).start()
        ring(0, 0, int_ref).start()
        ring(0, 1, int_ref).start()
        load_amp(1).wait()
        own(1).start()
        swap(0, 0, int_ref).start()
        load_amp(2).wait()
        own(2).start()

        tiles_own[SLOTS] = jnp.zeros((TILE, TILE), jnp.bfloat16)
        tiles_out[SLOTS] = jnp.zeros((TILE, TILE), jnp.bfloat16)
        make_table()
        tab_a = pltpu.make_async_copy(table_own, smem_own, l_tab.at[0])
        tab_a.start()
        tab_in().wait_recv()
        tab_b = pltpu.make_async_copy(table_out, smem_out, l_tab.at[1])
        tab_b.start()
        load_v.wait()
        tab_a.wait()
        tab_b.wait()
        for c in range(3, N):
            load_amp(c).wait()

        def compute(c, p, top=0, rows=TILE):
            width = WIDTHS[c]
            smem = (smem_own, smem_out)[p]
            target = (mine, done)[p][c]

            def pair(j, total):
                a, b = 2 * j, 2 * j + 1
                left = jnp.concatenate(
                    [tiles[p][smem[1, a], top : top + rows], tiles[p][smem[1, b], top : top + rows]], 1
                )
                right = jnp.concatenate([held[c][smem[0, a]], held[c][smem[0, b]]], 0)
                product = jnp.dot(left, right, preferred_element_type=jnp.float32)
                total = total * smem[2, j].astype(jnp.float32) + product
                prefix[j, 0:rows, 0:width] = total.astype(jnp.bfloat16)
                return total

            lax.fori_loop(0, PAIRS, pair, jnp.zeros((rows, width), jnp.float32), unroll=UNROLL_LAST if (c, p) == (N - 1, 1) else UNROLL)

            def place(b, carry):
                value = prefix[smem[3, b], 0:rows, 0:width].astype(jnp.float32)
                target[b, top : top + rows] = (value * smem[4, b].astype(jnp.float32)).astype(jnp.bfloat16)
                return carry

            lax.fori_loop(0, BLOCKS, place, 0)
            if p and rows < TILE:
                result_part(c, top, rows).start()
            elif p:
                result(c).start()
            else:
                pltpu.make_async_copy(target, columns(out_ref, c), l_out.at[c]).start()

        def issue_fwd(c):
            amp_in(c, partner_pos).wait_recv()
            fwd(c).start()

        def chunk_in(c):
            own_in(c).wait_recv()
            fwd_in(c).wait_recv()

        ring_come(0)
        v_in().wait_recv()
        ring(1, 0).start()
        ring(1, 1).start()
        swap(1, 0).start()
        own(0).wait_send()
        own(3).start()
        own(1).wait_send()
        issue_fwd(0)
        ring_come(1)
        ring_on(1)
        own(2).wait_send()
        issue_fwd(1)
        ring_end(1)
        ring_on(0)
        own(3).wait_send()
        issue_fwd(2)
        swap_end(1)
        chunk_in(0)
        compute(0, 1)
        ring_end(0)
        fwd(0).wait_send()
        issue_fwd(3)
        swap_end(0)
        chunk_in(1)
        compute(1, 1)
        compute(0, 0)
        fwd(1).wait_send()
        own(4).start()
        chunk_in(2)
        compute(2, 1)
        compute(1, 0)
        fwd(2).wait_send()
        issue_fwd(4)
        chunk_in(3)
        compute(3, 1)
        compute(2, 0)
        fwd(3).wait_send()

        @pl.when(core == 0)
        def _():
            own(5).start()

        compute(3, 0)
        own(4).wait_send()

        @pl.when(core == 0)
        def _():
            issue_fwd(5)

        chunk_in(4)

        @pl.when(core == 0)
        def _():
            own(5).wait_send()
            pl.semaphore_signal(turn_sem, inc=1, device_id=other, device_id_type=MESH)

        compute(4, 1)

        @pl.when(core == 1)
        def _():
            pl.semaphore_wait(turn_sem, 1)
            own(5).start()
            issue_fwd(5)

        compute(4, 0)
        chunk_in(5)
        compute(5, 1, 0, HALF)
        compute(5, 1, HALF, HALF)
        compute(5, 0)

        for k in range(2):
            result_part(N - 1, k * HALF, HALF).wait_send()
        fwd(4).wait_send()

        @pl.when(core == 1)
        def _():
            own(5).wait_send()

        fwd(5).wait_send()
        for p in range(2):
            for way in range(2):
                ring(p, way).wait_send()
                half(p, way).wait_send()
            for turn in range(YLEN):
                swap(p, turn).wait_send()
        for c in range(N):
            if c < N - 1:
                result(c).wait_send()
            pltpu.make_async_copy(mine[c], columns(out_ref, c), l_out.at[c]).wait()


def local(amplitudes, integrals, task_block, task_source, task_count):
    pair_count = amplitudes.shape[1]
    dma = pltpu.SemaphoreType.DMA
    bf16 = jnp.bfloat16
    chunks = [pltpu.VMEM((BLOCKS, TILE, w), bf16) for w in WIDTHS]
    scratch = [pltpu.VMEM((GROUP * BLOCKS, TILE, w), bf16) for w in WIDTHS] + chunks + chunks
    scratch += [
        pltpu.VMEM((SLOTS + 1, TILE, TILE), bf16),
        pltpu.VMEM((SLOTS + 1, TILE, TILE), bf16),
        pltpu.VMEM((PAIRS, TILE, max(WIDTHS)), bf16),
        pltpu.VMEM((8, ROW), jnp.int32),
        pltpu.VMEM((8, ROW), jnp.int32),
        pltpu.SMEM((8, ROW), jnp.int32),
        pltpu.SMEM((8, ROW), jnp.int32),
    ]
    scratch += [dma((N,))] * 10
    scratch += [dma((2, 2))] * 4 + [dma((2, YLEN))] * 2 + [dma] * 5 + [dma((2,)), pltpu.SemaphoreType.REGULAR]
    scratch += [pltpu.VMEM((1, SLOTS), jnp.int32)] * 2 + [dma((2,))] * 3
    in_hbm = functools.partial(pltpu.with_memory_space_constraint, memory_space=pltpu.HBM)
    any_space = pl.BlockSpec(memory_space=pl.ANY)
    smem = pl.BlockSpec(memory_space=pltpu.SMEM)
    result = pl.pallas_call(
        kernel,
        name="ladder",
        out_shape=pltpu.VMEM((BLOCKS, TILE, pair_count), bf16),
        in_specs=[any_space] * 4 + [smem],
        out_specs=any_space,
        scratch_shapes=scratch,
        compiler_params=pltpu.CompilerParams(
            collective_id=0, has_side_effects=True, vmem_limit_bytes=46 * 2**20
        ),
        cost_estimate=pl.CostEstimate(
            flops=4 * SLOTS * TILE * TILE * pair_count, bytes_accessed=8 * 2**20, transcendentals=0
        ),
    )(
        in_hbm(amplitudes.reshape(BLOCKS, TILE, pair_count)),
        in_hbm(integrals),
        in_hbm(task_block.reshape(1, SLOTS)),
        in_hbm(task_source.reshape(1, SLOTS)),
        task_count,
    )
    return result.reshape(BLOCKS * TILE, pair_count)


def solution(mesh):
    return jax.shard_map(
        local,
        mesh=mesh,
        in_specs=(P("vir", "occ"), P(("vir", "occ"), None, None), P("vir"), P("vir"), P("vir")),
        out_specs=P("vir", "occ"),
        check_vma=False,
    )
```

```python
import functools

import jax
import jax.numpy as jnp
from jax import lax
from jax.sharding import PartitionSpec as P
import jax.experimental.pallas as pl
import jax.experimental.pallas.tpu as pltpu

MESH = pl.DeviceIdType.MESH
ZLEN = 8
GROUP = 4
YLEN = 4
TILE = 128
HALF = TILE // 2
BLOCKS = 16
SLOTS = 256
SHARD = 32
PAIRS = (SLOTS + BLOCKS) // 2
ROW = 384
WIDTHS = (128,) * 6
STARTS = (0, 128, 256, 384, 512, 640)
N = len(WIDTHS)
UNROLL = 17
UNROLL_LAST = 68


def task_table(count, block, source):
    i32 = jnp.int32
    slot_l = lax.broadcasted_iota(i32, (SLOTS, SLOTS), 1)
    slot_s = lax.broadcasted_iota(i32, (SLOTS, SLOTS), 0)
    key_l = jnp.where(slot_l < count, jnp.broadcast_to(block, (SLOTS, SLOTS)), BLOCKS)
    key_s = key_l.T
    source_s = jnp.broadcast_to(source, (SLOTS, SLOTS)).T[:, 0:1]
    before = jnp.where((key_l == key_s) & (slot_l < slot_s), 1, 0)
    order = jnp.sum(before, axis=1, keepdims=True)
    key = key_s[:, 0:1]
    blk_s = lax.broadcasted_iota(i32, (BLOCKS, SLOTS), 0)
    n_s = jnp.sum(jnp.where(key_l[0:BLOCKS] == blk_s, 1, 0), axis=1, keepdims=True)
    even_s = ((n_s + 1) // 2) * 2
    lane = lax.broadcasted_iota(i32, (SLOTS, ROW), 1)
    n_l = jnp.sum(jnp.where(key == lane, 1, 0), axis=0, keepdims=True)
    n_l = jnp.where(lane[0:1] < BLOCKS, n_l, 0)
    even_l = ((n_l + 1) // 2) * 2
    lane16 = lax.broadcasted_iota(i32, (BLOCKS, ROW), 1)
    sub16 = lax.broadcasted_iota(i32, (BLOCKS, ROW), 0)
    base_l = jnp.sum(jnp.where(sub16 < lane16, even_s, 0), axis=0, keepdims=True)
    base_s = jnp.sum(jnp.where(lane16 < sub16, even_l, 0), axis=1, keepdims=True)
    base = jnp.sum(jnp.where(lane < key, even_l, 0), axis=1, keepdims=True)
    place = jnp.where(key < BLOCKS, base + order, ROW)
    here = place == lane
    slot = lax.broadcasted_iota(i32, (SLOTS, ROW), 0)
    amp = jnp.sum(jnp.where(here, source_s, 0), axis=0, keepdims=True)
    integral = SLOTS + jnp.sum(jnp.where(here, slot - SLOTS, 0), axis=0, keepdims=True)
    begins = jnp.where((base_s == 2 * lane16) & (n_s > 0), 1, 0)
    goes_on = 1 - jnp.sum(begins, axis=0, keepdims=True)
    last = jnp.maximum((base_l + even_l) // 2 - 1, 0)
    last = jnp.where(lane[0:1] < BLOCKS, last, 0)
    filled = jnp.where(n_l > 0, 1, 0)
    row = lax.broadcasted_iota(i32, (8, ROW), 0)
    out = jnp.where(row == 0, amp, 0)
    for k, value in ((1, integral), (2, goes_on), (3, last), (4, filled)):
        out = jnp.where(row == k, value, out)
    return out


def kernel(amp_ref, int_ref, block_hbm, source_hbm, count_ref, out_ref, *scratch):
    held = scratch[0:N]
    done = scratch[N : 2 * N]
    mine = scratch[2 * N : 3 * N]
    (tiles_own, tiles_out, prefix, table_own, table_out, smem_own, smem_out,
     s_own, r_own, s_fwd, r_fwd, s_amp, r_amp, s_res, r_res, l_amp, l_out,
     s_ring, r_ring, s_half, r_half, s_core, r_core, s_v, r_v, s_tab, r_tab,
     l_v, l_tab, turn_sem, block_ref, source_ref, l_list, s_part, r_part) = scratch[3 * N :]
    tiles = (tiles_own, tiles_out)

    vir = lax.axis_index("vir")
    occ = lax.axis_index("occ")
    pos = vir % GROUP
    first = vir - pos
    y, core = occ // 2, occ % 2
    inner = (pos == 1) | (pos == 2)
    partner_pos = jnp.where(pos < 2, 1 - pos, 5 - pos)
    partner = (first + partner_pos, occ)
    cross_pos = 3 - pos
    cross = (first + cross_pos, occ)
    cross_partner_pos = jnp.where(cross_pos < 2, 1 - cross_pos, 5 - cross_pos)
    y_up = (vir, ((y + 1) % YLEN) * 2 + core)
    y_down = (vir, ((y + 3) % YLEN) * 2 + core)
    other = (vir, y * 2 + 1 - core)

    def part(ref, where):
        return ref.at[pl.ds(where * BLOCKS, BLOCKS)]

    def shard(p, yy, cc, begin=0, size=SHARD):
        start = ((yy % YLEN) * 2 + cc) * SHARD + begin
        return tiles[p].at[pl.ds(start, size)]

    def columns(ref, c):
        return ref.at[:, :, pl.ds(STARTS[c], WIDTHS[c])]

    def send(src, dst, ssem, rsem, to):
        return pltpu.make_async_remote_copy(
            src_ref=src, dst_ref=dst, send_sem=ssem, recv_sem=rsem, device_id=to, device_id_type=MESH
        )

    barrier = pltpu.get_barrier_semaphore()
    lists = [
        pltpu.make_async_copy(block_hbm, block_ref, l_list.at[0]),
        pltpu.make_async_copy(source_hbm, source_ref, l_list.at[1]),
    ]

    def make_table():
        for copy in lists:
            copy.wait()
        table_own[...] = task_table(count_ref[0], block_ref[...], source_ref[...])

    def load_amp(c):
        return pltpu.make_async_copy(columns(amp_ref, c), part(held[c], pos), l_amp.at[c])

    def amp_in(c, where):
        return send(part(held[c], where), part(held[c], where), s_amp.at[c], r_amp.at[c], partner)

    def v_in():
        return send(int_ref, shard(1, y, core), s_v, r_v, partner)

    def tab_in():
        return send(table_own, table_out, s_tab, r_tab, partner)

    def result(c):
        return send(done[c], columns(out_ref, c), s_res.at[c], r_res.at[c], partner)

    def result_part(c, top, rows):
        k = top // rows
        return send(done[c].at[:, pl.ds(top, rows)], columns(out_ref, c).at[:, pl.ds(top, rows)],
                    s_part.at[k], r_part.at[k], partner)

    @pl.when(jnp.logical_not(inner))
    def _():
        pl.semaphore_signal(barrier, inc=1, device_id=partner, device_id_type=MESH)
        for c in range(N):
            load_amp(c).start()
        for copy in lists:
            copy.start()
        pl.semaphore_wait(barrier, 1)
        v_in().start()
        make_table()
        tab_in().start()
        v_in().wait_send()
        queue = []
        for c in range(N):
            load_amp(c).wait()
            if len(queue) > 1:
                queue.pop(0).wait_send()
            copy = amp_in(c, pos)
            copy.start()
            queue.append(copy)
        for copy in queue:
            copy.wait_send()
        tab_in().wait_send()
        for c in range(N - 1):
            result(c).wait_recv()
        for k in range(2):
            result_part(N - 1, k * HALF, HALF).wait_recv()

    @pl.when(inner)
    def _():
        for to in (partner, cross, y_up, y_down, other):
            pl.semaphore_signal(barrier, inc=1, device_id=to, device_id_type=MESH)
        for c in range(N):
            load_amp(c).start()
        load_v = pltpu.make_async_copy(int_ref, shard(0, y, core), l_v)
        load_v.start()
        for copy in lists:
            copy.start()
        pl.semaphore_wait(barrier, 5)

        def own(c):
            return send(part(held[c], pos), part(held[c], pos), s_own.at[c], r_own.at[c], cross)

        def own_in(c):
            return send(part(held[c], pos), part(held[c], cross_pos), s_own.at[c], r_own.at[c], cross)

        def fwd(c):
            return send(part(held[c], partner_pos), part(held[c], partner_pos), s_fwd.at[c], r_fwd.at[c], cross)

        def fwd_in(c):
            return send(part(held[c], partner_pos), part(held[c], cross_partner_pos), s_fwd.at[c], r_fwd.at[c], cross)

        def ring(p, way, src=None):
            src = shard(p, y, core) if src is None else src
            return send(src, shard(p, y, core), s_ring.at[p, way], r_ring.at[p, way], (y_up, y_down)[way])

        def ring_in(p, way):
            return send(shard(p, y, core), shard(p, y + (3, 1)[way], core), s_ring.at[p, way], r_ring.at[p, way],
                        (y_up, y_down)[way])

        def half(p, way):
            ref = shard(p, y + (3, 1)[way], core, way * (SHARD // 2), SHARD // 2)
            return send(ref, ref, s_half.at[p, way], r_half.at[p, way], (y_up, y_down)[way])

        def half_in(p, way):
            ref = shard(p, y + 2, core, way * (SHARD // 2), SHARD // 2)
            return send(ref, ref, s_half.at[p, way], r_half.at[p, way], (y_up, y_down)[way])

        def swap(p, turn, src=None):
            ref = shard(p, y + turn, core)
            return send(ref if src is None else src, ref, s_core.at[p, turn], r_core.at[p, turn], other)

        def swap_in(p, turn):
            return send(shard(p, y + turn, core), shard(p, y + turn, 1 - core), s_core.at[p, turn],
                        r_core.at[p, turn], other)

        def ring_come(p):
            for way in range(2):
                ring_in(p, way).wait_recv()
                swap(p, (3, 1)[way]).start()

        def ring_on(p):
            for way in range(2):
                half(p, way).start()

        def ring_end(p):
            for way in range(2):
                half_in(p, way).wait_recv()
            swap(p, 2).start()

        def swap_end(p):
            for turn in range(YLEN):
                swap_in(p, turn).wait_recv()

        load_amp(0).wait()
        own(0).start()
        ring(0, 0, int_ref).start()
        ring(0, 1, int_ref).start()
        load_amp(1).wait()
        own(1).start()
        swap(0, 0, int_ref).start()
        load_amp(2).wait()
        own(2).start()

        tiles_own[SLOTS] = jnp.zeros((TILE, TILE), jnp.bfloat16)
        tiles_out[SLOTS] = jnp.zeros((TILE, TILE), jnp.bfloat16)
        make_table()
        tab_a = pltpu.make_async_copy(table_own, smem_own, l_tab.at[0])
        tab_a.start()
        tab_in().wait_recv()
        tab_b = pltpu.make_async_copy(table_out, smem_out, l_tab.at[1])
        tab_b.start()
        load_v.wait()
        tab_a.wait()
        tab_b.wait()
        for c in range(3, N):
            load_amp(c).wait()

        def compute(c, p, top=0, rows=TILE):
            width = WIDTHS[c]
            smem = (smem_own, smem_out)[p]
            target = (mine, done)[p][c]

            def pair(j, total):
                a, b = 2 * j, 2 * j + 1
                left = jnp.concatenate(
                    [tiles[p][smem[1, a], top : top + rows], tiles[p][smem[1, b], top : top + rows]], 1
                )
                right = jnp.concatenate([held[c][smem[0, a]], held[c][smem[0, b]]], 0)
                product = jnp.dot(left, right, preferred_element_type=jnp.float32)
                total = total * smem[2, j].astype(jnp.float32) + product
                prefix[j, 0:rows, 0:width] = total.astype(jnp.bfloat16)
                return total

            lax.fori_loop(0, PAIRS, pair, jnp.zeros((rows, width), jnp.float32), unroll=UNROLL_LAST if (c, p) == (N - 1, 1) else UNROLL)

            def place(b, carry):
                value = prefix[smem[3, b], 0:rows, 0:width].astype(jnp.float32)
                target[b, top : top + rows] = (value * smem[4, b].astype(jnp.float32)).astype(jnp.bfloat16)
                return carry

            lax.fori_loop(0, BLOCKS, place, 0, unroll=BLOCKS)
            if p and rows < TILE:
                result_part(c, top, rows).start()
            elif p:
                result(c).start()
            else:
                pltpu.make_async_copy(target, columns(out_ref, c), l_out.at[c]).start()

        def issue_fwd(c):
            amp_in(c, partner_pos).wait_recv()
            fwd(c).start()

        def chunk_in(c):
            own_in(c).wait_recv()
            fwd_in(c).wait_recv()

        ring_come(0)
        v_in().wait_recv()
        ring(1, 0).start()
        ring(1, 1).start()
        swap(1, 0).start()
        own(0).wait_send()
        own(3).start()
        own(1).wait_send()
        issue_fwd(0)
        ring_come(1)
        ring_on(1)
        own(2).wait_send()
        issue_fwd(1)
        ring_end(1)
        ring_on(0)
        own(3).wait_send()
        issue_fwd(2)
        swap_end(1)
        chunk_in(0)
        compute(0, 1)
        ring_end(0)
        fwd(0).wait_send()
        issue_fwd(3)
        swap_end(0)
        chunk_in(1)
        compute(1, 1)
        compute(0, 0)
        fwd(1).wait_send()
        own(4).start()
        chunk_in(2)
        compute(2, 1)
        compute(1, 0)
        fwd(2).wait_send()
        issue_fwd(4)
        chunk_in(3)
        compute(3, 1)
        compute(2, 0)
        fwd(3).wait_send()

        @pl.when(core == 1)
        def _():
            own(5).start()

        compute(3, 0)
        own(4).wait_send()

        @pl.when(core == 1)
        def _():
            issue_fwd(5)

        chunk_in(4)

        @pl.when(core == 1)
        def _():
            own(5).wait_send()
            pl.semaphore_signal(turn_sem, inc=1, device_id=other, device_id_type=MESH)

        compute(4, 1)

        @pl.when(core == 0)
        def _():
            pl.semaphore_wait(turn_sem, 1)
            own(5).start()
            issue_fwd(5)

        compute(4, 0)
        chunk_in(5)
        compute(5, 1, 0, HALF)
        compute(5, 1, HALF, HALF)
        compute(5, 0)

        for k in range(2):
            result_part(N - 1, k * HALF, HALF).wait_send()
        fwd(4).wait_send()

        @pl.when(core == 0)
        def _():
            own(5).wait_send()

        fwd(5).wait_send()
        for p in range(2):
            for way in range(2):
                ring(p, way).wait_send()
                half(p, way).wait_send()
            for turn in range(YLEN):
                swap(p, turn).wait_send()
        for c in range(N):
            if c < N - 1:
                result(c).wait_send()
            pltpu.make_async_copy(mine[c], columns(out_ref, c), l_out.at[c]).wait()


def local(amplitudes, integrals, task_block, task_source, task_count):
    pair_count = amplitudes.shape[1]
    dma = pltpu.SemaphoreType.DMA
    bf16 = jnp.bfloat16
    chunks = [pltpu.VMEM((BLOCKS, TILE, w), bf16) for w in WIDTHS]
    scratch = [pltpu.VMEM((GROUP * BLOCKS, TILE, w), bf16) for w in WIDTHS] + chunks + chunks
    scratch += [
        pltpu.VMEM((SLOTS + 1, TILE, TILE), bf16),
        pltpu.VMEM((SLOTS + 1, TILE, TILE), bf16),
        pltpu.VMEM((PAIRS, TILE, max(WIDTHS)), bf16),
        pltpu.VMEM((8, ROW), jnp.int32),
        pltpu.VMEM((8, ROW), jnp.int32),
        pltpu.SMEM((8, ROW), jnp.int32),
        pltpu.SMEM((8, ROW), jnp.int32),
    ]
    scratch += [dma((N,))] * 10
    scratch += [dma((2, 2))] * 4 + [dma((2, YLEN))] * 2 + [dma] * 5 + [dma((2,)), pltpu.SemaphoreType.REGULAR]
    scratch += [pltpu.VMEM((1, SLOTS), jnp.int32)] * 2 + [dma((2,))] * 3
    in_hbm = functools.partial(pltpu.with_memory_space_constraint, memory_space=pltpu.HBM)
    any_space = pl.BlockSpec(memory_space=pl.ANY)
    smem = pl.BlockSpec(memory_space=pltpu.SMEM)
    result = pl.pallas_call(
        kernel,
        name="ladder",
        out_shape=pltpu.VMEM((BLOCKS, TILE, pair_count), bf16),
        in_specs=[any_space] * 4 + [smem],
        out_specs=any_space,
        scratch_shapes=scratch,
        compiler_params=pltpu.CompilerParams(
            collective_id=0, has_side_effects=True, vmem_limit_bytes=46 * 2**20
        ),
        cost_estimate=pl.CostEstimate(
            flops=4 * SLOTS * TILE * TILE * pair_count, bytes_accessed=8 * 2**20, transcendentals=0
        ),
    )(
        in_hbm(amplitudes.reshape(BLOCKS, TILE, pair_count)),
        in_hbm(integrals),
        in_hbm(task_block.reshape(1, SLOTS)),
        in_hbm(task_source.reshape(1, SLOTS)),
        task_count,
    )
    return result.reshape(BLOCKS * TILE, pair_count)


def solution(mesh):
    return jax.shard_map(
        local,
        mesh=mesh,
        in_specs=(P("vir", "occ"), P(("vir", "occ"), None, None), P("vir"), P("vir"), P("vir")),
        out_specs=P("vir", "occ"),
        check_vma=False,
    )
```
